32 devices in a mesh: expert: 4 (over y, x), ctx: 2 (over core), dp: 4 (over z).
Axes of the slice: x: 2, y: 2, z: 4, core: 2. Of those that a mesh axis runs over, the one named last changes fastest.
Arguments:
- prompt_tokens: bfloat16 [4, 1024, 2048], P('dp', 'ctx'), may hold values from -6 to 6
- sequel_tokens: bfloat16 [4, 2, 512, 2048], P('dp', None, 'ctx'), may hold values from -6 to 6
- attention_gain: float32 [2048], replicated, may hold values from 0.1 to 1.9
- query_weight: bfloat16 [2048, 4096], P(None, 'expert'), may hold values from -0.125 to 0.125
- key_weight: bfloat16 [2048, 512], replicated, may hold values from -0.125 to 0.125
- value_weight: bfloat16 [2048, 512], replicated, may hold values from -0.125 to 0.125
- query_gain: float32 [128], replicated, may hold values from 0.1 to 1.9
- key_gain: float32 [128], replicated, may hold values from 0.1 to 1.9
- out_weight: bfloat16 [4096, 2048], P('expert'), may hold values from -1.5 to 1.5
- feed_gain: float32 [2048], replicated, may hold values from 0.1 to 1.9
- router_weight: bfloat16 [2048, 16], replicated, may hold values from -0.0625 to 0.0625
- gate_up_weight: bfloat16 [16, 2048, 1536], P(('expert', 'dp')), may hold values from -0.125 to 0.125
- down_weight: bfloat16 [16, 768, 2048], P(('expert', 'dp')), may hold values from -0.875 to 0.875
- prompt_routes: int32 [4, 1024, 8], P('dp', 'ctx'), may hold values from 0 to 15, all different within a row; in each aligned block of 128 rows (0 to 127, 128 to 255, ..., all dimensions but the last counted through in order) at most 128 rows name the same one
- sequel_routes: int32 [4, 2, 512, 8], P('dp', None, 'ctx'), may hold values from 0 to 15, all different within a row; in each aligned block of 64 rows (0 to 63, 64 to 127, ..., all dimensions but the last counted through in order) at most 64 rows name the same one
- prompt_cotangent: bfloat16 [4, 1024, 2048], P('dp', 'ctx'), may hold values from -6 to 6
- sequel_cotangent: bfloat16 [4, 2, 512, 2048], P('dp', None, 'ctx'), may hold values from -6 to 6
Outputs:
- layer_prompt: bfloat16 [4, 1024, 2048], P('dp', 'ctx')
- layer_sequel: bfloat16 [4, 2, 512, 2048], P('dp', None, 'ctx')
- grad_prompt: bfloat16 [4, 1024, 2048], P('dp', 'ctx')
- grad_sequel: bfloat16 [4, 2, 512, 2048], P('dp', None, 'ctx')
- grad_attention_gain: float32 [2048], replicated
- grad_query: float32 [2048, 4096], P(None, 'expert')
- grad_key: float32 [2048, 512], replicated
- grad_value: float32 [2048, 512], replicated
- grad_query_gain: float32 [128], replicated
- grad_key_gain: float32 [128], replicated
- grad_out: float32 [4096, 2048], P('expert')
- grad_feed_gain: float32 [2048], replicated
- grad_router: float32 [2048, 16], replicated
- grad_gate_up: float32 [16, 2048, 1536], P(('expert', 'dp'))
- grad_down: float32 [16, 768, 2048], P(('expert', 'dp'))
The draws below stay inside these ranges and needn't reach their ends.
Inputs may be any that keep to these rules, and one draw needn't show every extreme that they name: `prompt_routes`: each row names 8 different experts. In each aligned block of 128 rows (all leading dimensions together, in order) no expert is named by more than 128 rows, and in some block one expert is named by exactly 128 rows. `sequel_routes`: each row names 8 different experts. In each aligned block of 64 rows (all leading dimensions together, in order) no expert is named by more than 64 rows, and in some block one expert is named by exactly 64 rows.
All inputs are finite; a program needn't handle non-finite values.
Results may differ from the reference program's by a relative error of at most 0.028.
Values may be sent and summed in bfloat16 or wider, within the bound.
No kernel may reach another device: no remote copies, remote signals or barrier semaphores. Data moves between devices by JAX's collectives and lax.ppermute only.
A program may use at most 512 MiB of HBM per device.

```python
import math
import jax
import jax.numpy as jnp
import numpy as np
from jax import lax

D = 2048
H = 32
KV = 4
HD = 128
FF = 768
TOP = 8
P_SIZE = 1024
C = 512
E = 16
MB = 4
PBE = 128
CBE = 64
MOSTP = 128
MOSTC = 64


def block_levels(key, dims, pieces, low, largest):
    def one(axis_at, shards_of):
        heights = jax.random.uniform(jax.random.fold_in(jax.random.fold_in(key, 6), axis_at), (shards_of,), jnp.float32, low / len(pieces), largest / len(pieces))
        return jnp.repeat(jnp.exp(heights), dims[axis_at] // shards_of).reshape((-1,) + (1,) * (len(dims) - axis_at - 1))

    factor_of = one(*pieces[0])
    for cut in pieces[1:]:
        factor_of = factor_of * one(*cut)
    return factor_of


def assign_block(key, own, number, rows, amount, top, reach, skew):
    order = jax.random.permutation(key, amount)
    crowded, common = shares(amount, rows * top, reach, skew, True), shares(amount, rows * top, reach, skew, False)
    places = jnp.arange(amount)

    def named(lengths, offset_by):
        used = int((lengths > 0).sum())
        fixed = max(1, used // 4)
        moved = fixed + (places - fixed + offset_by * (used - fixed)) % max(1, amount - fixed)
        return jnp.zeros((amount,), jnp.int32).at[order[jnp.where(places < fixed, places, moved)]].set(jnp.asarray(lengths, jnp.int32))

    lengths = jnp.where(number % 4 == 0, named(crowded, number // 4), named(common, number - number // 4 - 1))
    mixed = jax.random.permutation(jax.random.fold_in(own, 3), amount)
    giver, taker = mixed[0:amount // 2 * 2:2], mixed[1:amount // 2 * 2:2]
    margin = jnp.minimum(lengths[giver] - 1, reach - lengths[taker]) // 2
    margin = jnp.where((giver == order[0]) | (taker == order[0]) | (lengths[taker] == 0), 0, jnp.maximum(margin, 0))
    moved = jax.random.randint(jax.random.fold_in(own, 4), (amount // 2,), 0, 1 << 20) % (margin + 1)
    lengths = lengths.at[giver].add(-moved).at[taker].add(moved)
    members = jnp.searchsorted(jnp.cumsum(lengths), jnp.arange(rows * top), side="right").astype(jnp.int32)
    table = members.reshape(top, rows).T
    table = table[jax.random.permutation(jax.random.fold_in(own, 1), rows)]
    offset_by = jax.random.randint(jax.random.fold_in(own, 2), (rows, 1), 0, top)
    return jnp.take_along_axis(table, (jnp.arange(top)[None, :] + offset_by) % top, axis=1)


def shares(number_of, total, bound, slope, full):
    portions = [(1 << 20) // math.isqrt(standing ** slope) + 1 for standing in range(1, number_of + 1)]
    largest = bound if full else min(bound, max(-(-total // number_of), total * portions[0] // sum(portions)))
    least = 1 if total - largest >= number_of - 1 else 0
    holding, rest = [largest] + [least] * (number_of - 1), total - largest - least * (number_of - 1)
    while rest > 0:
        movable = [i for i in range(1, number_of) if holding[i] < largest] or [i for i in range(1, number_of) if holding[i] < bound]
        pool, budget = sum([portions[i] for i in movable]), rest
        for i in movable:
            more = min(bound - holding[i], max(1, budget * portions[i] // pool), rest)
            holding[i] = holding[i] + more
            rest = rest - more
    return np.array(holding)


def gaussian(key, dims, spread, most, cuts=(), held_as=jnp.bfloat16):
    array = spread * jax.random.normal(key, dims, jnp.float32)
    if cuts:
        array = array * block_levels(key, dims, cuts, -0.22, 0.18)
    return jnp.clip(array, -most, most).astype(held_as)


def setup_inputs(seed: int = 0) -> dict:
    key_list = jax.random.split(jax.random.key(seed), 18)
    prompt_tokens = gaussian(key_list[0], (MB, P_SIZE, D), 1.0, 6.0, ((0, 4), (1, 2)))
    sequel_tokens = gaussian(key_list[1], (MB, 2, C, D), 1.0, 6.0, ((0, 4), (2, 2)))
    attention_gain = jnp.clip(1.0 + 0.18 * jax.random.normal(key_list[2], (D,), jnp.float32), 0.1, 1.9)
    query_weight = gaussian(key_list[3], (D, H * HD), D ** -0.5, 0.125, ((1, 4),))
    key_weight = gaussian(key_list[4], (D, KV * HD), D ** -0.5, 0.125)
    value_weight = gaussian(key_list[5], (D, KV * HD), D ** -0.5, 0.125)
    query_gain = jnp.clip(1.0 + 0.18 * jax.random.normal(key_list[6], (HD,), jnp.float32), 0.1, 1.9)
    key_gain = jnp.clip(1.0 + 0.18 * jax.random.normal(key_list[7], (HD,), jnp.float32), 0.1, 1.9)
    out_weight = gaussian(key_list[8], (H * HD, D), (H * HD // 256) ** -0.5, 1.5, ((0, 4),))
    feed_gain = jnp.clip(1.0 + 0.18 * jax.random.normal(key_list[9], (D,), jnp.float32), 0.1, 1.9)
    router_weight = gaussian(key_list[10], (D, E), (4 * D) ** -0.5, 0.0625)
    gate_up_weight = gaussian(key_list[11], (E, D, 2 * FF), D ** -0.5, 0.125, ((0, 16),))
    down_weight = gaussian(key_list[12], (E, FF, D), (FF // 16) ** -0.5, 0.875, ((0, 16),))
    prompt_routes_keys = jax.random.split(jax.random.fold_in(key_list[13], 1), MB * P_SIZE // PBE)
    prompt_routes_turns = jax.random.permutation(jax.random.fold_in(key_list[13], 3), MB * P_SIZE // PBE)
    prompt_routes = jax.vmap(lambda own, number: assign_block(jax.random.fold_in(key_list[13], 2), own, number, PBE, E, TOP, MOSTP, 2))(prompt_routes_keys, prompt_routes_turns).reshape((MB, P_SIZE, TOP))
    sequel_routes_keys = jax.random.split(jax.random.fold_in(key_list[14], 1), MB * 2 * C // CBE)
    sequel_routes_turns = jax.random.permutation(jax.random.fold_in(key_list[14], 3), MB * 2 * C // CBE)
    sequel_routes = jax.vmap(lambda own, number: assign_block(jax.random.fold_in(key_list[14], 2), own, number, CBE, E, TOP, MOSTC, 2))(sequel_routes_keys, sequel_routes_turns).reshape((MB, 2, C, TOP))
    prompt_cotangent = gaussian(key_list[15], (MB, P_SIZE, D), 1.0, 6.0, ((0, 4), (1, 2)))
    sequel_cotangent = gaussian(key_list[16], (MB, 2, C, D), 1.0, 6.0, ((0, 4), (2, 2)))
    return {"prompt_tokens": prompt_tokens, "sequel_tokens": sequel_tokens, "attention_gain": attention_gain, "query_weight": query_weight, "key_weight": key_weight, "value_weight": value_weight, "query_gain": query_gain, "key_gain": key_gain, "out_weight": out_weight, "feed_gain": feed_gain, "router_weight": router_weight, "gate_up_weight": gate_up_weight, "down_weight": down_weight, "prompt_routes": prompt_routes, "sequel_routes": sequel_routes, "prompt_cotangent": prompt_cotangent, "sequel_cotangent": sequel_cotangent}


@jax.custom_vjp
def low(v):
    return lax.optimization_barrier(v.astype(jnp.bfloat16)).astype(jnp.float32)

@jax.custom_vjp
def low_back(v):
    return v

def low_keep(v):
    return (low(v), None)

def low_pass(kept, grad):
    return (grad,)

def back_keep(v):
    return (v, None)

def back_low(kept, grad):
    return (low(grad),)
low.defvjp(low_keep, low_pass)
low_back.defvjp(back_keep, back_low)
NORM_EPS = 1e-06
ROPE_BASE = 1000000.0
NEGATIVE_FILL = -1e+30
HIGHEST = lax.Precision.HIGHEST

def rms_scaled(values, gain_row):
    return values * lax.rsqrt(lax.optimization_barrier(jnp.mean(values * values, axis=-1, keepdims=True)) + NORM_EPS) * gain_row

def rotary_tables(positions, head_width):
    halfway = head_width // 2
    frequency = jnp.exp(jnp.arange(halfway, dtype=jnp.float32) * (-2.0 * math.log(ROPE_BASE) / head_width))
    angles = positions[:, None] * frequency[None, :]
    return (jnp.cos(angles), jnp.sin(angles))

def rotate(values, cosine, sine_table):
    halfway = values.shape[-1] // 2
    first_half = values[..., :halfway]
    second_half = values[..., halfway:]
    cos_rows = cosine[:, None, :]
    sin_rows = sine_table[:, None, :]
    return jnp.concatenate([first_half * cos_rows - second_half * sin_rows, second_half * cos_rows + first_half * sin_rows], axis=-1)

def layer(prompt_tokens, sequel_tokens, attention_gain, query_weight, key_weight, value_weight, query_gain, key_gain, out_weight, feed_gain, router_weight, gate_up_weight, down_weight, prompt_routes, sequel_routes):
    length = P_SIZE + 2 * C
    stacked = jnp.concatenate([prompt_tokens, sequel_tokens.reshape(MB, 2 * C, D)], axis=1)
    positions = jnp.concatenate([jnp.arange(P_SIZE), P_SIZE + jnp.arange(C), P_SIZE + jnp.arange(C)]).astype(jnp.float32)
    segments = jnp.concatenate([jnp.zeros(P_SIZE, jnp.int32), jnp.ones(C, jnp.int32), jnp.full((C,), 2, jnp.int32)])
    allowed = (positions[None, :] <= positions[:, None]) & ((segments[None, :] == 0) | (segments[None, :] == segments[:, None]))
    cosine, sine_table = rotary_tables(positions, HD)
    group_size = H // KV
    score_scale = 1.0 / math.sqrt(HD)

    def head_group(operands):
        query_heads, key_head, value_head = operands
        scores = low_back(jnp.einsum('gqd,td->gqt', query_heads, key_head, precision=HIGHEST) * score_scale)
        scores = jnp.where(allowed[None], scores, NEGATIVE_FILL)
        probabilities = low(jax.nn.softmax(scores, axis=-1))
        return jnp.einsum('gqt,td->gqd', probabilities, value_head, precision=HIGHEST)

    def attend(token_rows):
        hidden = low(rms_scaled(token_rows, attention_gain))
        query_pre = low_back(jnp.dot(hidden, query_weight, precision=HIGHEST)).reshape(length, H, HD)
        key_pre = low_back(jnp.dot(hidden, key_weight, precision=HIGHEST)).reshape(length, KV, HD)
        value_rows = low(low_back(jnp.dot(hidden, value_weight, precision=HIGHEST))).reshape(length, KV, HD)
        queries = low(rotate(rms_scaled(query_pre, query_gain), cosine, sine_table))
        key_rows = low(rotate(rms_scaled(key_pre, key_gain), cosine, sine_table))
        grouped = queries.reshape(length, KV, group_size, HD).transpose(1, 2, 0, 3)
        mixed_heads = lax.map(jax.checkpoint(head_group), (grouped, key_rows.transpose(1, 0, 2), value_rows.transpose(1, 0, 2)))
        mixed_heads = low(low_back(mixed_heads)).transpose(2, 0, 1, 3).reshape(length, H * HD)
        return token_rows + low_back(jnp.dot(mixed_heads, out_weight, precision=HIGHEST))
    residual = lax.map(jax.checkpoint(attend), stacked)
    token_rows = residual.reshape(MB * length, D)
    routes_all = jnp.concatenate([prompt_routes, sequel_routes.reshape(MB, 2 * C, TOP)], axis=1).reshape(MB * length, TOP)
    normed = low(rms_scaled(token_rows, feed_gain))
    logits = jnp.dot(normed, router_weight, precision=HIGHEST)
    chosen_mask = (routes_all[:, :, None] == jnp.arange(E, dtype=jnp.int32)[None, None, :]).astype(jnp.float32)
    chosen = jnp.einsum('tke,te->tk', chosen_mask, logits, precision=HIGHEST)
    gate_weights = jax.nn.softmax(chosen, axis=-1)
    dense_gates = jnp.einsum('tk,tke->te', gate_weights, chosen_mask, precision=HIGHEST)

    def expert_step(running_sum, operands):
        gate_up, down_matrix, column = operands
        routed = low_back(normed)
        gate_pre = low_back(jnp.dot(routed, gate_up, precision=HIGHEST))
        active = low(jax.nn.silu(gate_pre[:, :FF]) * gate_pre[:, FF:])
        result = low(low_back(jnp.dot(active, down_matrix, precision=HIGHEST)))
        return (running_sum + column[:, None] * result, None)
    mixture, unused = lax.scan(jax.checkpoint(expert_step), jnp.zeros_like(token_rows), (gate_up_weight, down_weight, dense_gates.T))
    final_rows = (token_rows + mixture).reshape(MB, length, D)
    return (final_rows[:, :P_SIZE], final_rows[:, P_SIZE:].reshape(MB, 2, C, D))

def reference(prompt_tokens, sequel_tokens, attention_gain, query_weight, key_weight, value_weight, query_gain, key_gain, out_weight, feed_gain, router_weight, gate_up_weight, down_weight, prompt_routes, sequel_routes, prompt_cotangent, sequel_cotangent):
    floats = jax.tree.map(lambda element: element.astype(jnp.float32), (prompt_tokens, sequel_tokens, attention_gain, query_weight, key_weight, value_weight, query_gain, key_gain, out_weight, feed_gain, router_weight, gate_up_weight, down_weight))

    def forward(*inputs):
        return layer(*inputs, prompt_routes, sequel_routes)
    outputs, pullback = jax.vjp(forward, *floats)
    gradients = pullback((prompt_cotangent.astype(jnp.float32), sequel_cotangent.astype(jnp.float32)))
    return (outputs[0].astype(jnp.bfloat16), outputs[1].astype(jnp.bfloat16), gradients[0].astype(jnp.bfloat16), gradients[1].astype(jnp.bfloat16), gradients[2], gradients[3], gradients[4], gradients[5], gradients[6], gradients[7], gradients[8], gradients[9], gradients[10], gradients[11], gradients[12])
```

```python
import functools
import math

import jax
import jax.numpy as jnp
from jax import lax
from jax.experimental import pallas as pl
from jax.experimental.pallas import tpu as pltpu
from jax.sharding import PartitionSpec as P

H = 32
KV = 4
P_SIZE = 1024


NORM_EPS = 1e-06
ROPE_BASE = 1000000.0
HIGHEST = lax.Precision.HIGHEST
LOG2E = math.log2(math.e)


def rms_scaled(values, gain_row):
    return (
        values * lax.rsqrt(jnp.mean(values * values, axis=-1, keepdims=True) + NORM_EPS) * gain_row
    )


def rms_backward(values, gain_row, upstream):
    inverse = lax.rsqrt(jnp.mean(values * values, axis=-1, keepdims=True) + NORM_EPS)
    unit_rows = values * inverse
    scaled = upstream * gain_row
    inner_mean = jnp.mean(scaled * unit_rows, axis=-1, keepdims=True)
    return (inverse * (scaled - unit_rows * inner_mean), upstream * unit_rows)


def rotary_tables(positions, head_width):
    halfway = head_width // 2
    frequency = jnp.exp(
        jnp.arange(halfway, dtype=jnp.float32) * (-2.0 * math.log(ROPE_BASE) / head_width)
    )
    angles = positions[:, None] * frequency[None, :]
    cosine, sine = jnp.cos(angles), jnp.sin(angles)
    return (jnp.concatenate([cosine, cosine], 1), jnp.concatenate([-sine, sine], 1))


def f32(values):
    return values.astype(jnp.float32)


def low(values):
    return values.astype(jnp.bfloat16)


def ring_gather(own, axis, size):
    held = [own]
    for _ in range(size - 1):
        held.append(lax.ppermute(held[-1], axis, [(j, (j + 1) % size) for j in range(size)]))
    return held


def ring_scatter(parts, axis, size):
    if size == 1:
        return f32(parts[0])
    total = parts[1]
    for s in range(2, size + 1):
        total = lax.ppermute(total, axis, [(j, (j + 1) % size) for j in range(size)])
        total = f32(total) + f32(parts[s % size])
        if s < size:
            total = total.astype(parts[0].dtype)
    return total


def cube_bits(size):
    return [1 << k for k in range(size.bit_length() - 1)]


def cube_gather(own, axis, size, bits):
    held = {0: own}
    for bit in bits:
        for r in list(held):
            held[r ^ bit] = lax.ppermute(held[r], axis, [(j, j ^ bit) for j in range(size)])
    return [held[r] for r in range(size)]


def cube_gather_halves(own, axis, size):
    half = own.shape[0] // 2
    bits = cube_bits(size)
    first = cube_gather(own[:half], axis, size, bits)
    second = cube_gather(own[half:], axis, size, bits[::-1])
    return list(zip(first, second))


def cube_scatter(parts, axis, size, bits):
    held = dict(enumerate(parts))
    for bit in bits:
        for r in [r for r in held if r & bit]:
            there = lax.ppermute(low(held.pop(r)), axis, [(j, j ^ bit) for j in range(size)])
            total = f32(held[r ^ bit]) + f32(there)
            held[r ^ bit] = total if bit == bits[-1] else low(total)
    return f32(held[0])


def cube_scatter_halves(parts, axis, size):
    half = parts[0].shape[0] // 2
    bits = cube_bits(size)
    first = cube_scatter([p[:half] for p in parts], axis, size, bits)
    second = cube_scatter([p[half:] for p in parts], axis, size, bits[::-1])
    return jnp.concatenate([first, second], axis=0)


def swap(values, axis):
    return lax.ppermute(values, axis, [(0, 1), (1, 0)])


def to_cube(rows, index, size):
    share = rows.shape[0] // size
    return jnp.concatenate(
        [lax.dynamic_slice_in_dim(rows, (index ^ r) * share, share, 0) for r in range(size)], axis=0
    )


def from_cube(blocks, index):
    share = sum(b.shape[0] for b in blocks[0])
    whole = jnp.zeros((len(blocks) * share,) + blocks[0][0].shape[1:], blocks[0][0].dtype)
    for r, pieces in enumerate(blocks):
        at = (index ^ r) * share
        for piece in pieces:
            whole = lax.dynamic_update_slice_in_dim(whole, piece, at, 0)
            at = at + piece.shape[0]
    return whole


def dot_nn(a,b): return lax.dot_general(a,b,(((1,),(0,)),((),())),preferred_element_type=jnp.float32)
def dot_nt(a,b): return lax.dot_general(a,b,(((1,),(1,)),((),())),preferred_element_type=jnp.float32)

def moe_kernel(n_units, halves, pieces, *refs):
    n_w = sum(len(p) for p in pieces)
    x_ref, u_ref, gates_ref, router_ref = refs[:4]
    w_refs = refs[4:4 + n_w]
    (mix_ref, row_ref, coef_ref, act_ref, dgu_ref, gu_buf, d_buf, mix_acc, row_acc, gg_acc, sems) = refs[-11:]
    unit = pl.program_id(0)
    width = d_buf.shape[1] // halves

    def copies(k, slot):
        base = sum(len(p) for p in pieces[:k])
        out = []
        for j, (kind, half, off, size) in enumerate(pieces[k]):
            if kind == 0:
                dst = gu_buf.at[slot, pl.ds(off, size), pl.ds(half * 2 * width, 2 * width)]
            else:
                dst = d_buf.at[slot, pl.ds(half * width + off, size)]
            out.append(pltpu.make_async_copy(w_refs[base + j], dst, sems.at[slot, j]))
        return out

    @pl.when(unit == 0)
    def _():
        for c in copies(0, 0):
            c.start()
        mix_acc[...] = jnp.zeros_like(mix_acc)
        row_acc[...] = jnp.zeros_like(row_acc)
        gg_acc[...] = jnp.zeros_like(gg_acc)

    for k in range(n_units):
        @pl.when(unit == k)
        def _(k=k):
            if k + 1 < n_units:
                for c in copies(k + 1, (k + 1) % 2):
                    c.start()
            for c in copies(k, k % 2):
                c.wait()

    slot = lax.rem(unit, 2)
    gates = gates_ref[...]
    lane = lax.broadcasted_iota(jnp.int32, gates.shape, 1)
    here = lane == unit
    gate = jnp.sum(jnp.where(here, gates, 0.0), axis=1, keepdims=True)
    x = x_ref[...]
    u = u_ref[...]
    acts, dgus = [], []
    gg = 0.0
    for h in range(halves):
        gu = gu_buf[slot, :, h * 2 * width:(h + 1) * 2 * width]
        d = d_buf[slot, h * width:(h + 1) * width]
        pre = dot_nn(x, gu)
        back = dot_nt(u, d)
        g_part = pre[:, :width]
        u_part = pre[:, width:]
        sig = 1.0 / (1.0 + jnp.exp(-g_part))
        silu = g_part * sig
        active = silu * u_part
        acts.append((active * gate).astype(jnp.bfloat16))
        gg = gg + jnp.sum(active * back, axis=1, keepdims=True)
        ag = back * gate
        dgus.append((ag * u_part * (sig + silu * (1.0 - sig))).astype(jnp.bfloat16))
        dgus.append((ag * silu).astype(jnp.bfloat16))
    act = jnp.concatenate(acts, axis=1)
    dgu = jnp.concatenate(dgus, axis=1)
    gg_acc[...] += jnp.where(here, gg, 0.0)
    act_ref[0] = act
    dgu_ref[0] = dgu
    mix_acc[...] += dot_nn(act, d_buf[slot])
    row_acc[...] += dot_nt(dgu, gu_buf[slot])

    @pl.when(unit == n_units - 1)
    def _():
        coef = gates * gg_acc[...]
        coef_ref[...] = coef
        mix_ref[...] = mix_acc[...].astype(jnp.bfloat16)
        extra = dot_nn(coef.astype(jnp.bfloat16), router_ref[...])
        row_ref[...] = (row_acc[...] + extra).astype(jnp.bfloat16)

def moe_rows(x, u, gates, router_rows, units, halves, slot_at, slots, kept):
    rows, width = x.shape
    n_units = len(units)
    pieces = [[(k, h, o, a.shape[0]) for k, h, o, a in unit] for unit in units]
    arrays = [a for unit in units for _, _, _, a in unit]
    hidden = sum(a.shape[0] for k, h, o, a in units[0] if k == 1)
    most = max(len(p) for p in pieces)
    any_spec = pl.BlockSpec(memory_space=pl.ANY)
    whole = lambda shape: pl.BlockSpec(shape, lambda i: (0,) * len(shape))
    in_specs = [whole(x.shape), whole(u.shape), whole(gates.shape), whole(router_rows.shape)] + [any_spec] * len(arrays)
    operands = [x, u, gates, router_rows] + arrays
    aliases = {}
    if kept is not None:
        in_specs += [any_spec, any_spec]
        aliases = {len(operands): 3, len(operands) + 1: 4}
        operands += list(kept)
    f32 = jnp.float32
    flops = 2 * rows * width * hidden * 6 * n_units
    return pl.pallas_call(
        functools.partial(moe_kernel, n_units, halves, pieces),
        grid=(n_units,),
        in_specs=in_specs,
        out_specs=[whole((rows, width)), whole((rows, width)), whole((rows, 128)),
            pl.BlockSpec((1, rows, hidden), lambda i: (i, slot_at, 0)),
            pl.BlockSpec((1, rows, 2 * hidden), lambda i: (i, slot_at, 0))],
        out_shape=[jax.ShapeDtypeStruct((rows, width), jnp.bfloat16), jax.ShapeDtypeStruct((rows, width), jnp.bfloat16),
            jax.ShapeDtypeStruct((rows, 128), f32),
            jax.ShapeDtypeStruct((n_units, slots * rows, hidden), jnp.bfloat16),
            jax.ShapeDtypeStruct((n_units, slots * rows, 2 * hidden), jnp.bfloat16)],
        scratch_shapes=[pltpu.VMEM((2, width, 2 * hidden), jnp.bfloat16), pltpu.VMEM((2, hidden, width), jnp.bfloat16),
            pltpu.VMEM((rows, width), f32), pltpu.VMEM((rows, width), f32), pltpu.VMEM((rows, 128), f32),
            pltpu.SemaphoreType.DMA((2, most))],
        input_output_aliases=aliases,
        compiler_params=pltpu.CompilerParams(vmem_limit_bytes=56 * 1024 * 1024, dimension_semantics=("arbitrary",)),
        cost_estimate=pl.CostEstimate(flops=flops, bytes_accessed=sum(a.size * 2 for a in arrays), transcendentals=0),
    )(*operands)


def key_row(t, block, prompt_blocks, segment, segment_rows):
    later = prompt_blocks * block + segment * segment_rows + (t - prompt_blocks) * block
    return pl.multiple_of(jnp.where(t < prompt_blocks, t * block, later), block)

def block_plan(own, block, prompt_blocks, own_prompt):
    at = pl.program_id(0)
    is_prompt = at < own_prompt
    full = jnp.where(is_prompt, own * own_prompt + at, prompt_blocks + own)
    return full, jnp.maximum(at - own_prompt, 0)

def turn(values, cosine, sine):
    half = values.shape[-1] // 2
    return values * cosine + jnp.concatenate([values[:, half:], values[:, :half]], axis=-1) * sine

def fwd_kernel(heads, block, prompt_blocks, own_prompt, segment_rows, scale,
               own_ref, pre_ref, gain_ref, cos_ref, sin_ref, k_ref, v_ref, q_ref, out_ref, lse_ref, acc):
    full, segment = block_plan(own_ref[0], block, prompt_blocks, own_prompt)
    width = k_ref.shape[1]
    cosine, sine, gain = cos_ref[...], sin_ref[...], gain_ref[...]
    for h in range(heads):
        pre = pre_ref[:, h * width:(h + 1) * width]
        unit = pre * lax.rsqrt(jnp.mean(pre * pre, axis=1, keepdims=True) + NORM_EPS) * gain
        q_ref[h] = (turn(unit, cosine, sine) * scale).astype(jnp.bfloat16)
    acc[...] = jnp.zeros_like(acc)

    def step(t, masked):
        first = key_row(t, block, prompt_blocks, segment, segment_rows)
        keys = k_ref[pl.ds(first, block)]
        values = jnp.concatenate([v_ref[pl.ds(first, block)], jnp.ones((block, width), jnp.bfloat16)], axis=1)
        for h in range(heads):
            p = jnp.exp2(dot_nt(q_ref[h], keys))
            if masked:
                p = jnp.where(lax.broadcasted_iota(jnp.int32, p.shape, 1) <= lax.broadcasted_iota(jnp.int32, p.shape, 0), p, 0.0)
            acc[h] += dot_nn(p.astype(jnp.bfloat16), values)

    @pl.loop(0, full)
    def _(t):
        step(t, False)
    step(full, True)
    for h in range(heads):
        total = acc[h, :, width:]
        out_ref[:, h * width:(h + 1) * width] = (acc[h, :, :width] / total).astype(jnp.bfloat16)
        lse_ref[h:h + 1] = jnp.log2(total).T[:1]

def bwd_kernel(heads, block, prompt_blocks, own_prompt, segment_rows, scale,
               own_ref, q_ref, k_ref, kt_ref, v_ref, lse_ref, out_ref, do_ref, pre_ref, gain_ref, cos_ref, sin_ref,
               dpre_ref, dk_ref, dv_ref, dgain_ref, acc, delta):
    full, segment = block_plan(own_ref[0], block, prompt_blocks, own_prompt)
    width = k_ref.shape[1]

    @pl.when(pl.program_id(0) == 0)
    def _():
        dk_ref[...] = jnp.zeros_like(dk_ref)
        dv_ref[...] = jnp.zeros_like(dv_ref)
        dgain_ref[...] = jnp.zeros_like(dgain_ref)

    for h in range(heads):
        cols = slice(h * width, (h + 1) * width)
        prod = out_ref[:, cols].astype(jnp.float32) * do_ref[:, cols].astype(jnp.float32)
        delta[h:h + 1] = jnp.sum(prod.T, axis=0, keepdims=True)
    acc[...] = jnp.zeros_like(acc)

    def step(t, masked):
        first = key_row(t, block, prompt_blocks, segment, segment_rows)
        rows = pl.ds(first, block)
        keys = k_ref[rows]
        kt = kt_ref[:, rows]
        values = v_ref[rows]
        dk = dv = 0.0
        for h in range(heads):
            q = q_ref[h]
            do = do_ref[:, h * width:(h + 1) * width]
            p = jnp.exp2(dot_nt(keys, q) - lse_ref[h:h + 1])
            if masked:
                p = jnp.where(lax.broadcasted_iota(jnp.int32, p.shape, 0) <= lax.broadcasted_iota(jnp.int32, p.shape, 1), p, 0.0)
            ds = (p * (dot_nt(values, do) - delta[h:h + 1])).astype(jnp.bfloat16)
            dv += dot_nn(p.astype(jnp.bfloat16), do)
            dk += dot_nn(ds, q)
            acc[h] += dot_nn(kt, ds)
        dk_ref[rows] += dk
        dv_ref[rows] += dv

    @pl.loop(0, full)
    def _(t):
        step(t, False)
    step(full, True)
    cosine, sine, gain = cos_ref[...], sin_ref[...], gain_ref[...]
    dgain = 0.0
    for h in range(heads):
        cols = slice(h * width, (h + 1) * width)
        turned = turn(acc[h].T * scale, cosine, -sine)
        pre = pre_ref[:, cols]
        inverse = lax.rsqrt(jnp.mean(pre * pre, axis=1, keepdims=True) + NORM_EPS)
        unit = pre * inverse
        scaled = turned * gain
        dpre_ref[:, cols] = (inverse * (scaled - unit * jnp.mean(scaled * unit, axis=1, keepdims=True))).astype(jnp.bfloat16)
        dgain = dgain + jnp.sum(turned * unit, axis=0, keepdims=True)
    dgain_ref[...] += dgain

def attend(own, pre, gain, cosine, sine, keys, values, block, prompt_total, heads):
    rows = pre.shape[0]
    head = keys.shape[1]
    width = heads * head
    own_prompt = rows // block - 2
    segment_rows = (keys.shape[0] - prompt_total) // 2
    scale = LOG2E / math.sqrt(head)
    whole = lambda shape: pl.BlockSpec(shape, lambda i, s: (0,) * len(shape))
    row = lambda w: pl.BlockSpec((block, w), lambda i, s: (i, 0))
    return pl.pallas_call(
        functools.partial(fwd_kernel, heads, block, prompt_total // block, own_prompt, segment_rows, scale),
        grid_spec=pltpu.PrefetchScalarGridSpec(
            num_scalar_prefetch=1, grid=(rows // block,),
            in_specs=[row(width), whole((1, head)), row(head), row(head), whole(keys.shape), whole(values.shape)],
            out_specs=[pl.BlockSpec((heads, block, head), lambda i, s: (0, i, 0)), row(width),
                       pl.BlockSpec((heads, block), lambda i, s: (0, i))],
            scratch_shapes=[pltpu.VMEM((heads, block, 2 * head), jnp.float32)]),
        out_shape=[jax.ShapeDtypeStruct((heads, rows, head), jnp.bfloat16), jax.ShapeDtypeStruct((rows, width), jnp.bfloat16),
                   jax.ShapeDtypeStruct((heads, rows), jnp.float32)],
        compiler_params=pltpu.CompilerParams(vmem_limit_bytes=40 * 1024 * 1024, dimension_semantics=("arbitrary",)),
        cost_estimate=pl.CostEstimate(flops=2 * rows * keys.shape[0] * width * 2, bytes_accessed=rows * width * 10, transcendentals=rows * keys.shape[0] * heads // 2),
    )(own, pre, gain, cosine, sine, keys, values)

def attend_back(own, q, keys, keys_t, values, lse, out, dout, pre, gain, cosine, sine, block, prompt_total):
    rows, width = out.shape
    head = keys.shape[1]
    heads = width // head
    own_prompt = rows // block - 2
    segment_rows = (keys.shape[0] - prompt_total) // 2
    whole = lambda shape: pl.BlockSpec(shape, lambda i, s: (0,) * len(shape))
    row = lambda w: pl.BlockSpec((block, w), lambda i, s: (i, 0))
    return pl.pallas_call(
        functools.partial(bwd_kernel, heads, block, prompt_total // block, own_prompt, segment_rows, 1.0 / math.sqrt(head)),
        grid_spec=pltpu.PrefetchScalarGridSpec(
            num_scalar_prefetch=1, grid=(rows // block,),
            in_specs=[pl.BlockSpec((heads, block, head), lambda i, s: (0, i, 0)), whole(keys.shape), whole(keys_t.shape), whole(values.shape),
                      pl.BlockSpec((heads, block), lambda i, s: (0, i)), row(width), row(width), row(width), whole((1, head)), row(head), row(head)],
            out_specs=[row(width), whole(keys.shape), whole(keys.shape), whole((1, head))],
            scratch_shapes=[pltpu.VMEM((heads, head, block), jnp.float32), pltpu.VMEM((heads, block), jnp.float32)]),
        out_shape=[jax.ShapeDtypeStruct((rows, width), jnp.bfloat16), jax.ShapeDtypeStruct(keys.shape, jnp.float32),
                   jax.ShapeDtypeStruct(keys.shape, jnp.float32), jax.ShapeDtypeStruct((1, head), jnp.float32)],
        compiler_params=pltpu.CompilerParams(vmem_limit_bytes=40 * 1024 * 1024, dimension_semantics=("arbitrary",)),
        cost_estimate=pl.CostEstimate(flops=2 * rows * keys.shape[0] * width * 5, bytes_accessed=rows * width * 12, transcendentals=rows * keys.shape[0] * heads // 2),
    )(own, q, keys, keys_t, values, lse, out, dout, pre, gain, cosine, sine)


def weight_units(gate_up, down, expert_parts, ctx_parts, ctx_index):
    hidden = down.shape[0]
    halves = 2 if ctx_parts == 2 else 1
    width = hidden // halves

    def half_of(which):
        gate = lax.dynamic_slice_in_dim(gate_up, which * width, width, 1)
        up = lax.dynamic_slice_in_dim(gate_up, hidden + which * width, width, 1)
        return (
            jnp.concatenate([gate, up], axis=1),
            lax.dynamic_slice_in_dim(down, which * width, width, 0),
        )

    if halves == 2:
        mine, other = half_of(ctx_index), half_of(1 - ctx_index)
    else:
        mine, other = (gate_up, down), None
    units = []
    downs = cube_gather_halves(mine[1], "expert", expert_parts)
    ups = cube_gather_halves(mine[0], "expert", expert_parts)
    for r in range(expert_parts):
        unit = []
        if r == 0:
            sides = [([mine[0]], [mine[1]])] + ([([other[0]], [other[1]])] if halves == 2 else [])
        else:
            sides = [(ups[r], downs[r])]
            if halves == 2:
                sides.append(([swap(a, "ctx") for a in ups[r]], [swap(a, "ctx") for a in downs[r]]))
        for h, (up_pieces, down_pieces) in enumerate(sides):
            for kind, pieces in ((0, up_pieces), (1, down_pieces)):
                at = 0
                for piece in pieces:
                    unit.append((kind, h, at, piece))
                    at += piece.shape[0]
        units.append(unit)
    return units, halves


def weight_grads(x_all, u_all, act_all, dgu_all, halves, expert_parts, ctx_index):
    rows = (((0,), (0,)), ((), ()))
    hidden = act_all.shape[2]
    width = hidden // halves
    ups, downs = [None] * expert_parts, [None] * expert_parts
    for r in reversed(range(expert_parts)):

        def grads(h):
            d_up = lax.dot_general(
                x_all, dgu_all[r, :, h * 2 * width : (h + 1) * 2 * width], rows, preferred_element_type=jnp.float32
            )
            d_down = lax.dot_general(
                act_all[r, :, h * width : (h + 1) * width], u_all, rows, preferred_element_type=jnp.float32
            )
            return d_up, d_down

        if halves == 2:
            sent = [swap(low(g), "ctx") for g in grads(1)]
            up, down = [low(g + f32(s)) for g, s in zip(grads(0), sent)]
        else:
            up, down = [low(g) for g in grads(0)]
        ups[r], downs[r] = up, down
    up = low(cube_scatter_halves(ups, "expert", expert_parts))
    down = low(cube_scatter_halves(downs, "expert", expert_parts))
    if halves == 1:
        return f32(lax.psum(up, "ctx")), f32(lax.psum(down, "ctx"))
    up_other, down_other = swap(up, "ctx"), swap(down, "ctx")
    first = ctx_index == 0
    up0, up1 = jnp.where(first, up, up_other), jnp.where(first, up_other, up)
    down0, down1 = jnp.where(first, down, down_other), jnp.where(first, down_other, down)
    return (
        f32(jnp.concatenate([up0[:, :width], up1[:, :width], up0[:, width:], up1[:, width:]], axis=1)),
        f32(jnp.concatenate([down0, down1], axis=0)),
    )


def on_device(
    prompt_tokens,
    sequel_tokens,
    attention_gain,
    query_weight,
    key_weight,
    value_weight,
    query_gain,
    key_gain,
    out_weight,
    feed_gain,
    router_weight,
    gate_up_weight,
    down_weight,
    prompt_routes,
    sequel_routes,
    prompt_cotangent,
    sequel_cotangent,
):
    expert_parts, ctx_parts, dp_parts = (lax.axis_size(a) for a in ("expert", "ctx", "dp"))
    expert_index, ctx_index, dp_index = (lax.axis_index(a) for a in ("expert", "ctx", "dp"))
    prompt_rows = prompt_tokens.shape[1]
    sequel_rows = sequel_tokens.shape[2]
    rows = prompt_rows + 2 * sequel_rows
    share = rows // expert_parts
    model_width = prompt_tokens.shape[2]
    head_dim = query_gain.shape[0]
    query_width = query_weight.shape[1]
    query_heads = query_width // head_dim
    kv_first = expert_index * query_heads // (H // KV)
    experts = router_weight.shape[1]
    assert query_heads <= H // KV and gate_up_weight.shape[0] == 1
    prompt_total, sequel_total = prompt_rows * ctx_parts, sequel_rows * ctx_parts
    contract_rows = (((0,), (0,)), ((), ()))
    contract_cols = (((1,), (1,)), ((), ()))

    def stacked(prompt, sequel):
        return jnp.concatenate([prompt[0], sequel[0, 0], sequel[0, 1]], axis=0)

    def my_share(whole):
        return lax.dynamic_slice_in_dim(whole, expert_index * share, share, 0)

    units, halves = weight_units(
        gate_up_weight[0], down_weight[0], expert_parts, ctx_parts, ctx_index
    )
    upstream_mine = my_share(stacked(prompt_cotangent, sequel_cotangent))
    routes_mine = my_share(stacked(prompt_routes, sequel_routes))
    u_slots = ring_gather(upstream_mine, "dp", dp_parts)
    route_slots = ring_gather(routes_mine, "dp", dp_parts)

    tokens_low = stacked(prompt_tokens, sequel_tokens)
    hidden = low(rms_scaled(f32(tokens_low), attention_gain))
    qkv_weight = jnp.concatenate(
        [query_weight]
        + [
            lax.dynamic_slice_in_dim(w, kv_first * head_dim, head_dim, 1)
            for w in (key_weight, value_weight)
        ],
        axis=1,
    )
    pre = jnp.dot(hidden, qkv_weight, preferred_element_type=jnp.float32)
    key_pre = pre[:, query_width : query_width + head_dim]
    index_row = jnp.arange(rows, dtype=jnp.int32)
    position = jnp.where(
        index_row < prompt_rows,
        ctx_index * prompt_rows + index_row,
        prompt_total + ctx_index * sequel_rows + (index_row - prompt_rows) % sequel_rows,
    )
    cosine, sine = rotary_tables(f32(position), head_dim)
    key_local = low(turn(rms_scaled(key_pre, key_gain), cosine, sine))
    kv_local = jnp.concatenate([key_local, low(pre[:, query_width + head_dim :])], axis=1)
    kv_slots = ring_gather(kv_local, "ctx", ctx_parts)

    def spans(slot):
        owner = lax.rem(ctx_index - slot + ctx_parts, ctx_parts)
        return (
            (owner * prompt_rows, prompt_rows),
            (prompt_total + owner * sequel_rows, sequel_rows),
            (prompt_total + sequel_total + owner * sequel_rows, sequel_rows),
        )

    kv_all = jnp.zeros((rows * ctx_parts, 2 * head_dim), jnp.bfloat16)
    for s, block in enumerate(kv_slots):
        at = 0
        for first, size in spans(s):
            kv_all = lax.dynamic_update_slice_in_dim(kv_all, block[at : at + size], first, 0)
            at += size
    keys, values = kv_all[:, :head_dim], kv_all[:, head_dim:]
    own = ctx_index.reshape(1).astype(jnp.int32)
    query_gain_row = query_gain.reshape(1, head_dim)
    queries, heads, lse = attend(
        own, pre, query_gain_row, cosine, sine, keys, values, sequel_rows, prompt_total, query_heads
    )
    heads_cube = to_cube(heads, expert_index, expert_parts)
    partial = low(jnp.dot(heads_cube, out_weight, preferred_element_type=jnp.float32))
    attention_share = cube_scatter_halves(
        [partial[r * share : (r + 1) * share] for r in range(expert_parts)], "expert", expert_parts
    )
    tokens_mine = f32(my_share(tokens_low))
    residual = tokens_mine + attention_share
    normed = low(rms_scaled(residual, feed_gain))

    lane = jnp.arange(128, dtype=jnp.int32)
    lane_expert = jnp.where(
        lane < experts,
        (expert_index ^ (lane % expert_parts)) * dp_parts + (dp_index + lane // expert_parts) % dp_parts,
        -1,
    )
    lane_hot = (jnp.arange(experts, dtype=jnp.int32)[:, None] == lane_expert[None, :]).astype(jnp.bfloat16)
    router_lanes = low(jnp.dot(router_weight, lane_hot, preferred_element_type=jnp.float32))
    router_rows = router_lanes.T

    def gates_of(x, routes):
        logits = jnp.dot(x, router_lanes, preferred_element_type=jnp.float32)
        named = jnp.any(routes[:, :, None] == lane_expert[None, None, :], axis=1)
        peak = jnp.max(jnp.where(named, logits, -jnp.inf), axis=-1, keepdims=True)
        weights = jnp.where(named, jnp.exp(logits - peak), 0.0)
        return weights / jnp.sum(weights, axis=-1, keepdims=True)

    x_slots = ring_gather(normed, "dp", dp_parts)
    gate_slots = [gates_of(x, routes) for x, routes in zip(x_slots, route_slots)]
    mixes, row_parts, coefs = [], [], []
    kept = None
    for s in range(dp_parts):
        mix, row, coef, *kept = moe_rows(
            x_slots[s], u_slots[s], gate_slots[s], router_rows, units, halves, s, dp_parts, kept
        )
        mixes.append(mix)
        row_parts.append(row)
        coefs.append(coef)
    row_sum = ring_scatter(row_parts, "dp", dp_parts)
    dot = ring_scatter([jnp.sum(coef, axis=1) for coef in coefs], "dp", dp_parts)
    mixture = ring_scatter(mixes, "dp", dp_parts)
    layer_share = low(residual + mixture)
    gates = gate_slots[0]
    gates_dot = gates * dot[:, None]
    normed_grad = row_sum - jnp.dot(gates_dot, f32(router_rows), precision=HIGHEST)
    residual_part, feed_terms = rms_backward(residual, feed_gain, normed_grad)
    residual_grad = f32(upstream_mine) + residual_part
    feed_gain_grad = jnp.sum(feed_terms, axis=0)
    residual_cube = cube_gather_halves(low(residual_grad), "expert", expert_parts)
    x_all = jnp.concatenate(x_slots, axis=0)
    u_all = jnp.concatenate(u_slots, axis=0)
    coef_all = jnp.concatenate([coefs[0] - gates_dot] + coefs[1:], axis=0)
    router_grad = jnp.dot(
        lax.dot_general(f32(x_all), coef_all, contract_rows, precision=HIGHEST), f32(lane_hot).T, precision=HIGHEST
    )
    gate_up_grad, down_grad = weight_grads(
        x_all, u_all, kept[0], kept[1], halves, expert_parts, ctx_index
    )

    residual_low = jnp.concatenate([piece for pieces in residual_cube for piece in pieces], axis=0)
    heads_grad_cube = low(
        lax.dot_general(residual_low, out_weight, contract_cols, preferred_element_type=jnp.float32)
    )
    heads_grad = from_cube(
        [[heads_grad_cube[r * share : (r + 1) * share]] for r in range(expert_parts)], expert_index
    )
    out_weight_grad = lax.dot_general(
        heads_cube, residual_low, contract_rows, preferred_element_type=jnp.float32
    )
    query_low, key_grads, value_grads, query_gain_grad = attend_back(
        own, queries, keys, keys.T, values, lse, heads, heads_grad, pre, query_gain_row, cosine, sine,
        sequel_rows, prompt_total,
    )
    kv_grads = low(jnp.concatenate([key_grads * (1.0 / LOG2E), value_grads], axis=1))
    kv_sum = ring_scatter(
        [
            jnp.concatenate([lax.dynamic_slice_in_dim(kv_grads, a, n, 0) for a, n in spans(s)], axis=0)
            for s in range(ctx_parts)
        ],
        "ctx",
        ctx_parts,
    )
    key_turned = turn(kv_sum[:, :head_dim], cosine, -sine)
    key_pre_grad, key_terms = rms_backward(key_pre, key_gain, key_turned)
    key_gain_grad = jnp.sum(key_terms, axis=0)
    low_grads = jnp.concatenate([query_low, low(key_pre_grad), low(kv_sum[:, head_dim:])], axis=1)
    hidden_grad = low(
        lax.dot_general(
            to_cube(low_grads, expert_index, expert_parts), qkv_weight, contract_cols, preferred_element_type=jnp.float32
        )
    )
    hidden_grad_mine = cube_scatter_halves(
        [hidden_grad[r * share : (r + 1) * share] for r in range(expert_parts)], "expert", expert_parts
    )
    qkv_grad = lax.dot_general(hidden, low_grads, contract_rows, preferred_element_type=jnp.float32)
    input_part, attention_terms = rms_backward(tokens_mine, attention_gain, hidden_grad_mine)
    attention_gain_grad = jnp.sum(attention_terms, axis=0)
    input_share = low(residual_grad + input_part)

    out_total = f32(lax.psum(low(out_weight_grad), ("ctx", "dp")))
    qkv_total = lax.psum(low(qkv_grad), ("ctx", "dp"))
    query_total = f32(qkv_total[:, :query_width])
    kv_total = qkv_total[:, query_width:]
    if expert_parts == KV:
        kv_cube = cube_gather(kv_total, "expert", expert_parts, cube_bits(expert_parts))
    else:
        kv_cube = None
    kv_outs = []
    for part in range(2):
        whole = jnp.zeros((model_width, KV * head_dim), jnp.float32)
        cols = slice(part * head_dim, (part + 1) * head_dim)
        if kv_cube is not None:
            for r in range(expert_parts):
                whole = lax.dynamic_update_slice_in_dim(
                    whole, f32(kv_cube[r][:, cols]), (expert_index ^ r) * head_dim, 1
                )
        else:
            whole = lax.dynamic_update_slice_in_dim(whole, f32(kv_total[:, cols]), kv_first * head_dim, 1)
            whole = f32(lax.psum(low(whole), "expert"))
        kv_outs.append(whole)
    everywhere = ("expert", "ctx", "dp")
    router_total, feed_total = lax.psum((router_grad, feed_gain_grad), everywhere)
    attention_total, query_gain_total, key_gain_total = lax.psum(
        (attention_gain_grad, query_gain_grad.reshape(head_dim), key_gain_grad), everywhere
    )
    layer_full = from_cube(cube_gather_halves(layer_share, "expert", expert_parts), expert_index)
    input_full = from_cube(cube_gather_halves(input_share, "expert", expert_parts), expert_index)

    def split(whole):
        return (
            whole[:prompt_rows][None],
            whole[prompt_rows:].reshape(1, 2, sequel_rows, model_width),
        )

    return (
        *split(layer_full),
        *split(input_full),
        attention_total,
        query_total,
        kv_outs[0],
        kv_outs[1],
        query_gain_total,
        key_gain_total,
        out_total,
        feed_total,
        router_total,
        gate_up_grad[None],
        down_grad[None],
    )


def solution(mesh):
    placed = (
        P("dp", "ctx", None),
        P("dp", None, "ctx", None),
        P(),
        P(None, "expert"),
        P(),
        P(),
        P(),
        P(),
        P("expert", None),
        P(),
        P(),
        P(("expert", "dp"), None, None),
        P(("expert", "dp"), None, None),
        P("dp", "ctx", None),
        P("dp", None, "ctx", None),
        P("dp", "ctx", None),
        P("dp", None, "ctx", None),
    )
    return jax.shard_map(
        on_device,
        mesh=mesh,
        in_specs=placed,
        out_specs=(
            P("dp", "ctx", None),
            P("dp", None, "ctx", None),
            P("dp", "ctx", None),
            P("dp", None, "ctx", None),
            P(),
            P(None, "expert"),
            P(),
            P(),
            P(),
            P(),
            P("expert", None),
            P(),
            P(),
            P(("expert", "dp"), None, None),
            P(("expert", "dp"), None, None),
        ),
        check_vma=False,
    )
```

```python
import functools
import math

import jax
import jax.numpy as jnp
from jax import lax
from jax.experimental import pallas as pl
from jax.experimental.pallas import tpu as pltpu
from jax.sharding import PartitionSpec as P

H = 32
KV = 4
P_SIZE = 1024


NORM_EPS = 1e-06
ROPE_BASE = 1000000.0
HIGHEST = lax.Precision.HIGHEST
LOG2E = math.log2(math.e)


def rms_scaled(values, gain_row):
    return (
        values * lax.rsqrt(jnp.mean(values * values, axis=-1, keepdims=True) + NORM_EPS) * gain_row
    )


def rms_backward(values, gain_row, upstream):
    inverse = lax.rsqrt(jnp.mean(values * values, axis=-1, keepdims=True) + NORM_EPS)
    unit_rows = values * inverse
    scaled = upstream * gain_row
    inner_mean = jnp.mean(scaled * unit_rows, axis=-1, keepdims=True)
    return (inverse * (scaled - unit_rows * inner_mean), upstream * unit_rows)


def rotary_tables(positions, head_width):
    halfway = head_width // 2
    frequency = jnp.exp(
        jnp.arange(halfway, dtype=jnp.float32) * (-2.0 * math.log(ROPE_BASE) / head_width)
    )
    angles = positions[:, None] * frequency[None, :]
    cosine, sine = jnp.cos(angles), jnp.sin(angles)
    return (jnp.concatenate([cosine, cosine], 1), jnp.concatenate([-sine, sine], 1))


def f32(values):
    return values.astype(jnp.float32)


def low(values):
    return values.astype(jnp.bfloat16)


def ring_gather(own, axis, size):
    held = [own]
    for _ in range(size - 1):
        held.append(lax.ppermute(held[-1], axis, [(j, (j + 1) % size) for j in range(size)]))
    return held


def ring_scatter(parts, axis, size):
    if size == 1:
        return f32(parts[0])
    total = parts[1]
    for s in range(2, size + 1):
        total = lax.ppermute(total, axis, [(j, (j + 1) % size) for j in range(size)])
        total = f32(total) + f32(parts[s % size])
        if s < size:
            total = total.astype(parts[0].dtype)
    return total


def cube_bits(size):
    return [1 << k for k in range(size.bit_length() - 1)]


def cube_gather(own, axis, size, bits):
    held = {0: own}
    for bit in bits:
        for r in list(held):
            held[r ^ bit] = lax.ppermute(held[r], axis, [(j, j ^ bit) for j in range(size)])
    return [held[r] for r in range(size)]


def cube_scatter(parts, axis, size, bits):
    held = dict(enumerate(parts))
    for bit in bits:
        for r in [r for r in held if r & bit]:
            there = lax.ppermute(low(held.pop(r)), axis, [(j, j ^ bit) for j in range(size)])
            total = f32(held[r ^ bit]) + f32(there)
            held[r ^ bit] = total if bit == bits[-1] else low(total)
    return f32(held[0])


def plane_hop(values, second):
    return lax.ppermute(
        values, ("expert", "ctx"), [(2 * j + c, 2 * (j ^ (1 if c == second else 2)) + c) for j in range(4) for c in range(2)]
    )


def plane_gather(own, quick, size):
    if not quick:
        return cube_gather(own, "expert", size, cube_bits(size))
    near = plane_hop(own, 0)
    return [own, near, plane_hop(own, 1), plane_hop(near, 1)]


def plane_scatter(blocks, quick, size, *hold):
    share = blocks.shape[0] // size
    if not quick:
        return cube_scatter(
            [blocks[r * share : (r + 1) * share] for r in range(size)], "expert", size, cube_bits(size)
        ), blocks
    came = plane_hop(blocks[2 * share :], 1)
    near = low(f32(blocks[share : 2 * share]) + f32(came[share:]))
    if hold:
        near = after(near, *hold)
    return f32(blocks[:share]) + f32(came[:share]) + f32(plane_hop(near, 0)), near


def sign(values):
    return values[:16, :128]


def after(value, *others):
    others = [sign(o) for o in others]
    anywhere = pl.BlockSpec(memory_space=pl.ANY)
    return pl.pallas_call(
        lambda *refs: None,
        in_specs=[anywhere] * (1 + len(others)),
        out_specs=anywhere,
        out_shape=jax.ShapeDtypeStruct(value.shape, value.dtype),
        input_output_aliases={0: 0},
    )(value, *others)


def butterfly(values, axes):
    for axis in axes:
        size = lax.axis_size(axis)
        for bit in cube_bits(size):
            values = values + lax.ppermute(values, axis, [(j, j ^ bit) for j in range(size)])
    return values


def swap(values, axis):
    return lax.ppermute(values, axis, [(0, 1), (1, 0)])


def to_slots(rows, order):
    share = rows.shape[0] // len(order)
    return jnp.concatenate([lax.dynamic_slice_in_dim(rows, at * share, share, 0) for at in order], axis=0)


def from_slots(rows, order):
    share = rows.shape[0] // len(order)
    whole = jnp.zeros_like(rows)
    for u, at in enumerate(order):
        whole = lax.dynamic_update_slice_in_dim(whole, rows[u * share : (u + 1) * share], at * share, 0)
    return whole


def dot_nn(a, b):
    return lax.dot_general(a, b, (((1,), (0,)), ((), ())), preferred_element_type=jnp.float32)


def dot_nt(a, b):
    return lax.dot_general(a, b, (((1,), (1,)), ((), ())), preferred_element_type=jnp.float32)


def moe_kernel(n_units, pieces, turned, half_ref, *refs):
    n_w = sum(len(p) for p in pieces)
    x_ref, u_ref, gates_ref, router_ref = refs[:4]
    w_refs = refs[4 : 4 + n_w]
    mix_ref, row_ref, coef_ref, act_ref, dgu_ref = refs[-11 - turned : -6 - turned]
    gu_buf, d_buf, mix_acc, row_acc, gg_acc, sems = refs[-6:]
    unit = pl.program_id(0)
    hidden = act_ref.shape[2]

    def copies(k, slot):
        base = sum(len(p) for p in pieces[:k])
        out = []
        for j, (kind, off, size) in enumerate(pieces[k]):
            if isinstance(off, str):
                off = pl.multiple_of((half_ref[0] if off == "mine" else 1 - half_ref[0]) * size, size)
            buf = d_buf if kind else gu_buf
            out.append(pltpu.make_async_copy(w_refs[base + j], buf.at[slot, pl.ds(off, size)], sems.at[slot, j]))
        return out

    @pl.when(unit == 0)
    def _():
        for c in copies(0, 0):
            c.start()
        mix_acc[...] = jnp.zeros_like(mix_acc)
        row_acc[...] = jnp.zeros_like(row_acc)
        gg_acc[...] = jnp.zeros_like(gg_acc)
        if turned:
            refs[-7][...] = x_ref[...].T

    for k in range(n_units):

        @pl.when(unit == k)
        def _(k=k):
            if k + 1 < n_units:
                for c in copies(k + 1, (k + 1) % 2):
                    c.start()
            for c in copies(k, k % 2):
                c.wait()

    slot = lax.rem(unit, 2)
    gates = gates_ref[...]
    lane = lax.broadcasted_iota(jnp.int32, gates.shape, 1)
    here = lane == unit
    gate = jnp.sum(jnp.where(here, gates, 0.0), axis=1, keepdims=True)
    gu = gu_buf[slot]
    down = d_buf[slot]
    back = dot_nt(u_ref[...], down)
    pre = dot_nn(x_ref[...], gu)
    g_part = pre[:, :hidden]
    u_part = pre[:, hidden:]
    sig = 1.0 / (1.0 + jnp.exp(-g_part))
    silu = g_part * sig
    active = silu * u_part
    act = (active * gate).astype(jnp.bfloat16)
    act_ref[0] = act
    gg_acc[...] += jnp.where(here, jnp.sum(active * back, axis=1, keepdims=True), 0.0)
    ag = back * gate
    dg = (ag * u_part * (sig + silu * (1.0 - sig))).astype(jnp.bfloat16)
    dgu = jnp.concatenate([dg, (ag * silu).astype(jnp.bfloat16)], axis=1)
    dgu_ref[0] = dgu
    mix_acc[...] += dot_nn(act, down)
    row_acc[...] += dot_nt(dgu, gu)

    @pl.when(unit == n_units - 1)
    def _():
        coef = gates * gg_acc[...]
        coef = coef - gates * jnp.sum(coef, axis=1, keepdims=True)
        coef_ref[...] = coef
        mix_ref[...] = mix_acc[...].astype(jnp.bfloat16)
        extra = dot_nn(coef.astype(jnp.bfloat16), router_ref[...])
        row_ref[...] = (row_acc[...] + extra).astype(jnp.bfloat16)


def moe_rows(places, x, u, gates, router_rows, units, slots, kept, others):
    rows, width = x.shape
    n_units = len(units)
    pieces = [[(k, o, a.shape[0]) for k, o, a in unit] for unit in units]
    arrays = [a for unit in units for _, _, a in unit]
    hidden = arrays[0].shape[1] // 2
    most = max(len(p) for p in pieces)
    anywhere = pl.BlockSpec(memory_space=pl.ANY)
    turned = int(rows % 128 == 0)

    def whole(shape):
        return pl.BlockSpec(shape, lambda i, s: (0,) * len(shape))

    others = [sign(o) for o in others]
    operands = [places, x, u, gates, router_rows] + arrays + others
    in_specs = [whole(x.shape), pl.BlockSpec((rows, width), lambda i, s: (0, 0))]
    in_specs += [whole(gates.shape), whole(router_rows.shape)]
    in_specs += [anywhere] * (len(arrays) + len(others))
    aliases = {}
    if kept is not None:
        aliases = {len(operands) + k: 3 + k for k in range(len(kept))}
        in_specs += [anywhere] * len(kept)
        operands += list(kept)
    return pl.pallas_call(
        functools.partial(moe_kernel, n_units, pieces, turned),
        grid_spec=pltpu.PrefetchScalarGridSpec(
            num_scalar_prefetch=1,
            grid=(n_units,),
            in_specs=in_specs,
            out_specs=[
                whole((rows, width)),
                whole((rows, width)),
                whole((rows, 128)),
                pl.BlockSpec((1, rows, hidden), lambda i, s: (i, s[1], 0)),
                pl.BlockSpec((1, rows, 2 * hidden), lambda i, s: (i, s[1], 0)),
                pl.BlockSpec((width, rows), lambda i, s: (0, s[1])),
            ][: 5 + turned],
            scratch_shapes=[
                pltpu.VMEM((2, width, 2 * hidden), jnp.bfloat16),
                pltpu.VMEM((2, hidden, width), jnp.bfloat16),
                pltpu.VMEM((rows, width), jnp.float32),
                pltpu.VMEM((rows, width), jnp.float32),
                pltpu.VMEM((rows, 128), jnp.float32),
                pltpu.SemaphoreType.DMA((2, most)),
            ],
        ),
        out_shape=[
            jax.ShapeDtypeStruct((rows, width), jnp.bfloat16),
            jax.ShapeDtypeStruct((rows, width), jnp.bfloat16),
            jax.ShapeDtypeStruct((rows, 128), jnp.float32),
            jax.ShapeDtypeStruct((n_units, slots * rows, hidden), jnp.bfloat16),
            jax.ShapeDtypeStruct((n_units, slots * rows, 2 * hidden), jnp.bfloat16),
            jax.ShapeDtypeStruct((width, slots * rows), jnp.bfloat16),
        ][: 5 + turned],
        input_output_aliases=aliases,
        compiler_params=pltpu.CompilerParams(
            vmem_limit_bytes=56 * 1024 * 1024, dimension_semantics=("arbitrary",)
        ),
        cost_estimate=pl.CostEstimate(
            flops=2 * rows * width * hidden * 6 * n_units,
            bytes_accessed=sum(a.size * 2 for a in arrays),
            transcendentals=rows * hidden * n_units,
        ),
    )(*operands)


def grad_kernel(width, with_sum, core_ref, *refs):
    xt_ref, ut_ref, dgu_ref, act_ref = refs[:4]
    out_ref = refs[-1]
    up = dot_nn(xt_ref[...], dgu_ref[0])
    down = dot_nn(ut_ref[...], act_ref[0])
    if with_sum:
        up = up + refs[4][:, : 2 * width].astype(jnp.float32)
        down = down + refs[4][:, 2 * width :].astype(jnp.float32)
    out_ref[:, : 2 * width] = up.astype(jnp.bfloat16)
    out_ref[:, 2 * width :] = down.astype(jnp.bfloat16)


def packed_grads(core, xt, ut, dgu, act, unit, other_half, added, others):
    model, rows = xt.shape
    width = act.shape[2]
    tile = min(512, model // 2)
    tiles = model // 2 // tile
    others = [sign(o) for o in others]
    operands = [core, xt, ut, dgu, act] + ([added] if added is not None else []) + others
    row = pl.BlockSpec((tile, rows), lambda i, s: (((1 - s[0]) if other_half else s[0]) * tiles + i, 0))
    packed = pl.BlockSpec((tile, 3 * width), lambda i, s: (i, 0))
    return pl.pallas_call(
        functools.partial(grad_kernel, width, added is not None),
        grid_spec=pltpu.PrefetchScalarGridSpec(
            num_scalar_prefetch=1,
            grid=(tiles,),
            in_specs=[
                row,
                row,
                pl.BlockSpec((1, rows, 2 * width), lambda i, s: (unit, 0, 0)),
                pl.BlockSpec((1, rows, width), lambda i, s: (unit, 0, 0)),
            ]
            + ([packed] if added is not None else [])
            + [pl.BlockSpec(memory_space=pl.ANY)] * len(others),
            out_specs=packed,
        ),
        out_shape=jax.ShapeDtypeStruct((model // 2, 3 * width), jnp.bfloat16),
        compiler_params=pltpu.CompilerParams(
            vmem_limit_bytes=48 * 1024 * 1024, dimension_semantics=("arbitrary",)
        ),
        cost_estimate=pl.CostEstimate(
            flops=rows * model * 3 * width, bytes_accessed=model * rows * 2 + model * width * 3, transcendentals=0
        ),
    )(*operands)


def key_row(t, block, prompt_blocks, segment, segment_rows):
    later = prompt_blocks * block + segment * segment_rows + (t - prompt_blocks) * block
    return pl.multiple_of(jnp.where(t < prompt_blocks, t * block, later), block)

def block_plan(own, block, prompt_blocks, own_prompt):
    at = pl.program_id(0)
    is_prompt = at < own_prompt
    full = jnp.where(is_prompt, own * own_prompt + at, prompt_blocks + own)
    return full, jnp.maximum(at - own_prompt, 0)

def turn(values, cosine, sine):
    half = values.shape[-1] // 2
    return values * cosine + jnp.concatenate([values[:, half:], values[:, :half]], axis=-1) * sine

def fwd_kernel(heads, block, prompt_blocks, own_prompt, segment_rows, scale,
               own_ref, pre_ref, gain_ref, cos_ref, sin_ref, k_ref, v_ref, *rest):
    q_ref, out_ref, lse_ref, acc = rest[-4:]
    full, segment = block_plan(own_ref[0], block, prompt_blocks, own_prompt)
    width = k_ref.shape[1]
    cosine, sine, gain = cos_ref[...], sin_ref[...], gain_ref[...]
    for h in range(heads):
        pre = pre_ref[:, h * width:(h + 1) * width]
        unit = pre * lax.rsqrt(jnp.mean(pre * pre, axis=1, keepdims=True) + NORM_EPS) * gain
        q_ref[h] = (turn(unit, cosine, sine) * scale).astype(jnp.bfloat16)
    acc[...] = jnp.zeros_like(acc)

    def step(t, masked):
        first = key_row(t, block, prompt_blocks, segment, segment_rows)
        keys = k_ref[pl.ds(first, block)]
        values = jnp.concatenate([v_ref[pl.ds(first, block)], jnp.ones((block, width), jnp.bfloat16)], axis=1)
        for h in range(heads):
            p = jnp.exp2(dot_nt(q_ref[h], keys))
            if masked:
                p = jnp.where(lax.broadcasted_iota(jnp.int32, p.shape, 1) <= lax.broadcasted_iota(jnp.int32, p.shape, 0), p, 0.0)
            acc[h] += dot_nn(p.astype(jnp.bfloat16), values)

    @pl.loop(0, full)
    def _(t):
        step(t, False)
    step(full, True)
    for h in range(heads):
        total = acc[h, :, width:]
        out_ref[:, h * width:(h + 1) * width] = (acc[h, :, :width] / total).astype(jnp.bfloat16)
        lse_ref[h:h + 1] = jnp.log2(total).T[:1]

def bwd_kernel(heads, block, prompt_blocks, own_prompt, segment_rows, scale,
               own_ref, q_ref, k_ref, kt_ref, v_ref, lse_ref, out_ref, do_ref, pre_ref, gain_ref, cos_ref, sin_ref, *rest):
    dpre_ref, dk_ref, dv_ref, dgain_ref, acc, delta = rest[-6:]
    full, segment = block_plan(own_ref[0], block, prompt_blocks, own_prompt)
    width = k_ref.shape[1]

    @pl.when(pl.program_id(0) == 0)
    def _():
        dk_ref[...] = jnp.zeros_like(dk_ref)
        dv_ref[...] = jnp.zeros_like(dv_ref)
        dgain_ref[...] = jnp.zeros_like(dgain_ref)

    for h in range(heads):
        cols = slice(h * width, (h + 1) * width)
        prod = out_ref[:, cols].astype(jnp.float32) * do_ref[:, cols].astype(jnp.float32)
        delta[h:h + 1] = jnp.sum(prod.T, axis=0, keepdims=True)
    acc[...] = jnp.zeros_like(acc)

    def step(t, masked):
        first = key_row(t, block, prompt_blocks, segment, segment_rows)
        rows = pl.ds(first, block)
        keys = k_ref[rows]
        kt = kt_ref[:, rows]
        values = v_ref[rows]
        dk = dv = 0.0
        for h in range(heads):
            q = q_ref[h]
            do = do_ref[:, h * width:(h + 1) * width]
            p = jnp.exp2(dot_nt(keys, q) - lse_ref[h:h + 1])
            if masked:
                p = jnp.where(lax.broadcasted_iota(jnp.int32, p.shape, 0) <= lax.broadcasted_iota(jnp.int32, p.shape, 1), p, 0.0)
            ds = (p * (dot_nt(values, do) - delta[h:h + 1])).astype(jnp.bfloat16)
            dv += dot_nn(p.astype(jnp.bfloat16), do)
            dk += dot_nn(ds, q)
            acc[h] += dot_nn(kt, ds)
        dk_ref[rows] += dk
        dv_ref[rows] += dv

    @pl.loop(0, full)
    def _(t):
        step(t, False)
    step(full, True)
    cosine, sine, gain = cos_ref[...], sin_ref[...], gain_ref[...]
    dgain = 0.0
    for h in range(heads):
        cols = slice(h * width, (h + 1) * width)
        turned = turn(acc[h].T * scale, cosine, -sine)
        pre = pre_ref[:, cols]
        inverse = lax.rsqrt(jnp.mean(pre * pre, axis=1, keepdims=True) + NORM_EPS)
        unit = pre * inverse
        scaled = turned * gain
        dpre_ref[:, cols] = (inverse * (scaled - unit * jnp.mean(scaled * unit, axis=1, keepdims=True))).astype(jnp.bfloat16)
        dgain = dgain + jnp.sum(turned * unit, axis=0, keepdims=True)
    dgain_ref[...] += dgain

def attend(own, pre, gain, cosine, sine, keys, values, block, prompt_total, heads, others):
    rows = pre.shape[0]
    head = keys.shape[1]
    width = heads * head
    own_prompt = rows // block - 2
    segment_rows = (keys.shape[0] - prompt_total) // 2
    scale = LOG2E / math.sqrt(head)
    whole = lambda shape: pl.BlockSpec(shape, lambda i, s: (0,) * len(shape))
    row = lambda w: pl.BlockSpec((block, w), lambda i, s: (i, 0))
    moved = lambda w: pl.BlockSpec((block, w), lambda i, s: (s[1 + i], 0))
    return pl.pallas_call(
        functools.partial(fwd_kernel, heads, block, prompt_total // block, own_prompt, segment_rows, scale),
        grid_spec=pltpu.PrefetchScalarGridSpec(
            num_scalar_prefetch=1, grid=(rows // block,),
            in_specs=[row(width), whole((1, head)), row(head), row(head), whole(keys.shape), whole(values.shape)]
                     + [pl.BlockSpec(memory_space=pl.ANY)] * len(others),
            out_specs=[pl.BlockSpec((heads, block, head), lambda i, s: (0, i, 0)), moved(width),
                       pl.BlockSpec((heads, block), lambda i, s: (0, i))],
            scratch_shapes=[pltpu.VMEM((heads, block, 2 * head), jnp.float32)]),
        out_shape=[jax.ShapeDtypeStruct((heads, rows, head), jnp.bfloat16), jax.ShapeDtypeStruct((rows, width), jnp.bfloat16),
                   jax.ShapeDtypeStruct((heads, rows), jnp.float32)],
        compiler_params=pltpu.CompilerParams(vmem_limit_bytes=40 * 1024 * 1024, dimension_semantics=("arbitrary",)),
        cost_estimate=pl.CostEstimate(flops=2 * rows * keys.shape[0] * width * 2, bytes_accessed=rows * width * 10, transcendentals=rows * keys.shape[0] * heads // 2),
    )(own, pre, gain, cosine, sine, keys, values, *[sign(o) for o in others])

def attend_back(own, q, keys, keys_t, values, lse, out, dout, pre, gain, cosine, sine, block, prompt_total, others):
    rows, width = out.shape
    head = keys.shape[1]
    heads = width // head
    own_prompt = rows // block - 2
    segment_rows = (keys.shape[0] - prompt_total) // 2
    whole = lambda shape: pl.BlockSpec(shape, lambda i, s: (0,) * len(shape))
    row = lambda w: pl.BlockSpec((block, w), lambda i, s: (i, 0))
    moved = lambda w: pl.BlockSpec((block, w), lambda i, s: (s[1 + i], 0))
    return pl.pallas_call(
        functools.partial(bwd_kernel, heads, block, prompt_total // block, own_prompt, segment_rows, 1.0 / math.sqrt(head)),
        grid_spec=pltpu.PrefetchScalarGridSpec(
            num_scalar_prefetch=1, grid=(rows // block,),
            in_specs=[pl.BlockSpec((heads, block, head), lambda i, s: (0, i, 0)), whole(keys.shape), whole(keys_t.shape), whole(values.shape),
                      pl.BlockSpec((heads, block), lambda i, s: (0, i)), moved(width), moved(width), row(width), whole((1, head)), row(head), row(head)]
                     + [pl.BlockSpec(memory_space=pl.ANY)] * len(others),
            out_specs=[row(width), whole(keys.shape), whole(keys.shape), whole((1, head))],
            scratch_shapes=[pltpu.VMEM((heads, head, block), jnp.float32), pltpu.VMEM((heads, block), jnp.float32)]),
        out_shape=[jax.ShapeDtypeStruct((rows, width), jnp.bfloat16), jax.ShapeDtypeStruct(keys.shape, jnp.float32),
                   jax.ShapeDtypeStruct(keys.shape, jnp.float32), jax.ShapeDtypeStruct((1, head), jnp.float32)],
        compiler_params=pltpu.CompilerParams(vmem_limit_bytes=40 * 1024 * 1024, dimension_semantics=("arbitrary",)),
        cost_estimate=pl.CostEstimate(flops=2 * rows * keys.shape[0] * width * 5, bytes_accessed=rows * width * 12, transcendentals=rows * keys.shape[0] * heads // 2),
    )(own, q, keys, keys_t, values, lse, out, dout, pre, gain, cosine, sine, *[sign(o) for o in others])


def plane_units(near, far, near_down, gate_up, down, ctx_index, hold):
    far_down = after(swap(near_down, "ctx"), hold)
    mine = [
        plane_hop(lax.dynamic_slice_in_dim(w, ctx_index * (w.shape[0] // 2), w.shape[0] // 2, 0), 0)
        for w in (far, far_down)
    ]
    return [
        [(0, 0, gate_up), (1, 0, down)],
        [(0, 0, near), (1, 0, near_down)],
        [(0, 0, far), (1, 0, far_down)],
        [(k, "mine", w) for k, w in enumerate(mine)] + [(k, "other", swap(w, "ctx")) for k, w in enumerate(mine)],
    ]


def unpack_kernel(core_ref, a_ref, b_ref, up_ref, down_ref):
    total = a_ref[...].astype(jnp.float32) + b_ref[...].astype(jnp.float32)
    width = total.shape[1] // 3
    up_ref[0] = total[:, : 2 * width]
    down_ref[0] = total[:, 2 * width :].T


def unpacked(core, own, came, half, outs):
    rows, packed = own.shape
    width = packed // 3
    tile = min(256, rows)
    tiles = rows // tile

    def at(i, s):
        return (s[0] if half == 0 else 1 - s[0]) * tiles + i

    anywhere = pl.BlockSpec(memory_space=pl.ANY)
    block = pl.BlockSpec((tile, packed), lambda i, s: (i, 0))
    return pl.pallas_call(
        (lambda c, a, b, *refs: unpack_kernel(c, a, b, *refs[-2:])),
        grid_spec=pltpu.PrefetchScalarGridSpec(
            num_scalar_prefetch=1,
            grid=(tiles,),
            in_specs=[block, block] + [anywhere] * len(outs),
            out_specs=[
                pl.BlockSpec((1, tile, 2 * width), lambda i, s: (0, at(i, s), 0)),
                pl.BlockSpec((1, width, tile), lambda i, s: (0, 0, at(i, s))),
            ],
        ),
        out_shape=[
            jax.ShapeDtypeStruct((1, 2 * rows, 2 * width), jnp.float32),
            jax.ShapeDtypeStruct((1, width, 2 * rows), jnp.float32),
        ],
        input_output_aliases={3 + k: k for k in range(len(outs))},
        compiler_params=pltpu.CompilerParams(
            vmem_limit_bytes=40 * 1024 * 1024, dimension_semantics=("arbitrary",)
        ),
        cost_estimate=pl.CostEstimate(flops=rows * packed, bytes_accessed=rows * packed * 8, transcendentals=0),
    )(core, own, came, *outs)


def place_kernel(order_ref, *refs):
    prompt_ref, sequel_ref = refs[-2:]
    at = pl.program_id(0)
    slot = order_ref[at]
    for u in range(4):

        @pl.when((slot == u) & (at < 2))
        def _(u=u):
            prompt_ref[0] = refs[u][...]

        @pl.when((slot == u) & (at >= 2))
        def _(u=u):
            sequel_ref[0, 0] = refs[u][...]


def place_rows(pieces, quick, order, slot_of, prompt_rows, sequel_rows):
    width = pieces[0].shape[1]
    if not quick:
        whole = from_slots(jnp.concatenate(pieces, axis=0), order)
        return whole[:prompt_rows][None], whole[prompt_rows:].reshape(1, 2, sequel_rows, width)
    share = pieces[0].shape[0]
    first = pl.BlockSpec((share, width), lambda i, s: (0, 0))
    return pl.pallas_call(
        place_kernel,
        grid_spec=pltpu.PrefetchScalarGridSpec(
            num_scalar_prefetch=1,
            grid=(4,),
            in_specs=[first] * 4,
            out_specs=[
                pl.BlockSpec((1, share, width), lambda i, s: (0, jnp.minimum(i, 1), 0)),
                pl.BlockSpec((1, 1, share, width), lambda i, s: (0, jnp.maximum(i - 2, 0), 0, 0)),
            ],
        ),
        out_shape=[
            jax.ShapeDtypeStruct((1, prompt_rows, width), pieces[0].dtype),
            jax.ShapeDtypeStruct((1, 2, sequel_rows, width), pieces[0].dtype),
        ],
        compiler_params=pltpu.CompilerParams(dimension_semantics=("arbitrary",)),
        cost_estimate=pl.CostEstimate(flops=0, bytes_accessed=16 * share * width, transcendentals=0),
    )(slot_of, *pieces)


def core_half(values, ctx_index):
    half = values.shape[0] // 2
    mine, other = (lax.dynamic_slice_in_dim(values, c * half, half, 0) for c in (ctx_index, 1 - ctx_index))
    return low(f32(mine) + f32(swap(other, "ctx")))


def both_halves(mine, ctx_index):
    other = swap(mine, "ctx")
    return jnp.concatenate(
        [jnp.where(ctx_index == 0, mine, other), jnp.where(ctx_index == 0, other, mine)], axis=0
    )


def on_device(
    prompt_tokens,
    sequel_tokens,
    attention_gain,
    query_weight,
    key_weight,
    value_weight,
    query_gain,
    key_gain,
    out_weight,
    feed_gain,
    router_weight,
    gate_up_weight,
    down_weight,
    prompt_routes,
    sequel_routes,
    prompt_cotangent,
    sequel_cotangent,
):
    expert_parts, ctx_parts, dp_parts = (lax.axis_size(a) for a in ("expert", "ctx", "dp"))
    expert_index, ctx_index, dp_index = (lax.axis_index(a) for a in ("expert", "ctx", "dp"))
    prompt_rows = prompt_tokens.shape[1]
    sequel_rows = sequel_tokens.shape[2]
    rows = prompt_rows + 2 * sequel_rows
    share = rows // expert_parts
    model_width = prompt_tokens.shape[2]
    head_dim = query_gain.shape[0]
    query_width = query_weight.shape[1]
    query_heads = query_width // head_dim
    kv_first = expert_index * query_heads // (H // KV)
    experts = router_weight.shape[1]
    assert query_heads <= H // KV and gate_up_weight.shape[0] == 1
    prompt_total, sequel_total = prompt_rows * ctx_parts, sequel_rows * ctx_parts
    contract_rows = (((0,), (0,)), ((), ()))
    contract_cols = (((1,), (1,)), ((), ()))

    def stacked(prompt, sequel):
        return jnp.concatenate([prompt[0], sequel[0, 0], sequel[0, 1]], axis=0)

    def my_share(whole):
        return lax.dynamic_slice_in_dim(whole, expert_index * share, share, 0)

    quick = expert_parts == 4 and ctx_parts == 2 and share == sequel_rows

    def turn_of(u):
        return jnp.where(ctx_index == 1, (u & 1) * 2 + (u >> 1), u) if quick else u

    order = [expert_index ^ turn_of(u) for u in range(expert_parts)]
    core = ctx_index.reshape(1).astype(jnp.int32)
    core = core if ctx_parts == 2 else 0 * core

    if quick:
        near_down = plane_hop(down_weight[0], 0)
        near_gate_up = plane_hop(gate_up_weight[0], 0)
    else:
        gathered = [cube_gather(w[0], "expert", expert_parts, cube_bits(expert_parts)) for w in (gate_up_weight, down_weight)]
        units = [[(0, 0, a), (1, 0, b)] for a, b in zip(*gathered)]
    tokens_low = stacked(prompt_tokens, sequel_tokens)
    hidden = low(rms_scaled(f32(tokens_low), attention_gain))
    upstream_mine = my_share(stacked(prompt_cotangent, sequel_cotangent))
    routes_mine = my_share(stacked(prompt_routes, sequel_routes))
    choices = routes_mine.shape[1]
    u_packed = jnp.concatenate([upstream_mine, jnp.pad(low(routes_mine), ((0, 0), (0, 128 - choices)))], axis=1)
    u_slots = ring_gather(after(u_packed, hidden), "dp", dp_parts)
    owners = [lax.rem(dp_index - s + dp_parts, dp_parts) for s in range(dp_parts)]

    qkv_weight = jnp.concatenate(
        [query_weight]
        + [
            lax.dynamic_slice_in_dim(w, kv_first * head_dim, head_dim, 1)
            for w in (key_weight, value_weight)
        ],
        axis=1,
    )
    pre = jnp.dot(hidden, qkv_weight, preferred_element_type=jnp.float32)
    key_pre = pre[:, query_width : query_width + head_dim]
    index_row = jnp.arange(rows, dtype=jnp.int32)
    position = jnp.where(
        index_row < prompt_rows,
        ctx_index * prompt_rows + index_row,
        prompt_total + ctx_index * sequel_rows + (index_row - prompt_rows) % sequel_rows,
    )
    cosine, sine = rotary_tables(f32(position), head_dim)
    key_local = low(turn(rms_scaled(key_pre, key_gain), cosine, sine))
    kv_local = jnp.concatenate([key_local, low(pre[:, query_width + head_dim :])], axis=1)
    if quick:
        kv_local = after(kv_local, u_slots[1])
    kv_slots = ring_gather(kv_local, "ctx", ctx_parts)

    def spans(slot):
        owner = lax.rem(ctx_index - slot + ctx_parts, ctx_parts)
        return (
            (owner * prompt_rows, prompt_rows),
            (prompt_total + owner * sequel_rows, sequel_rows),
            (prompt_total + sequel_total + owner * sequel_rows, sequel_rows),
        )

    kv_all = jnp.zeros((rows * ctx_parts, 2 * head_dim), jnp.bfloat16)
    for s, block in enumerate(kv_slots):
        at = 0
        for first, size in spans(s):
            kv_all = lax.dynamic_update_slice_in_dim(kv_all, block[at : at + size], first, 0)
            at += size
    keys, values = kv_all[:, :head_dim], kv_all[:, head_dim:]
    slot_of = jnp.stack([turn_of(expert_index ^ j) for j in range(expert_parts)]).astype(jnp.int32)
    storage = slot_of if quick else jnp.arange(rows // sequel_rows, dtype=jnp.int32)
    own = jnp.concatenate([ctx_index.reshape(1).astype(jnp.int32), storage])
    query_gain_row = query_gain.reshape(1, head_dim)
    queries, heads, lse = attend(
        own, pre, query_gain_row, cosine, sine, keys, values, sequel_rows, prompt_total, query_heads, []
    )
    heads_slots = heads if quick else to_slots(heads, order)
    partial = low(jnp.dot(heads_slots, out_weight, preferred_element_type=jnp.float32))
    if quick:
        partial = after(partial, near_gate_up, near_down, u_slots[2])
    attention_share, unused = plane_scatter(partial, quick, expert_parts, *u_slots[3:])
    tokens_mine = f32(my_share(tokens_low))
    residual = tokens_mine + attention_share
    normed = low(rms_scaled(residual, feed_gain))
    route_slots = [u[:, model_width : model_width + choices].astype(jnp.int32) for u in u_slots]

    lane = jnp.arange(128, dtype=jnp.int32)
    lane_expert = jnp.where(
        lane < experts,
        (expert_index ^ turn_of(lane % expert_parts)) * dp_parts + (dp_index + lane // expert_parts) % dp_parts,
        -1,
    )
    lane_hot = (jnp.arange(experts, dtype=jnp.int32)[:, None] == lane_expert[None, :]).astype(jnp.bfloat16)
    router_lanes = low(jnp.dot(router_weight, lane_hot, preferred_element_type=jnp.float32))
    router_rows = router_lanes.T

    def gates_of(x, routes):
        logits = jnp.dot(x, router_lanes, preferred_element_type=jnp.float32)
        named = jnp.any(routes[:, :, None] == lane_expert[None, None, :], axis=1)
        peak = jnp.max(jnp.where(named, logits, -jnp.inf), axis=-1, keepdims=True)
        weights = jnp.where(named, jnp.exp(logits - peak), 0.0)
        return weights / jnp.sum(weights, axis=-1, keepdims=True)

    def onward(total):
        return lax.ppermute(total, "dp", [(j, (j + 1) % dp_parts) for j in range(dp_parts)])

    x_slots = [normed]
    for _ in range(dp_parts - 1):
        x_slots.append(onward(x_slots[-1]))
    if quick:
        near_gate_up = after(near_gate_up, heads)
        far_gate_up = after(swap(near_gate_up, "ctx"), normed)
        units = plane_units(near_gate_up, far_gate_up, near_down, gate_up_weight[0], down_weight[0], ctx_index, x_slots[1])
    def rows_of(s, kept, others):
        return moe_rows(
            jnp.concatenate([core, owners[s].reshape(1).astype(jnp.int32)]),
            x_slots[s], u_slots[s], gates_of(x_slots[s], route_slots[s]), router_rows, units, dp_parts, kept, others,
        )

    mixes, coefs = ([None] * dp_parts for _ in range(2))
    kept, others, row_sum = None, [], None
    for s in [*range(1, dp_parts), 0]:
        mixes[s], row, coefs[s], *kept = rows_of(s, kept, others)
        if row_sum is not None:
            row = f32(row) + f32(onward(row_sum))
        row_sum = low(row) if s else f32(row)
        others = [row_sum] if s > 1 else []
    act_all, dgu_all = kept[:2]
    xt_all = kept[2] if len(kept) == 3 else from_slots(jnp.concatenate(x_slots, axis=0), owners).T
    u_all = after(jnp.concatenate([u[:, :model_width] for u in u_slots], axis=0), row_sum)
    ut_all = from_slots(u_all, owners).T

    def expert_grads(unit, other_half, added, *others):
        return packed_grads(core, xt_all, ut_all, dgu_all, act_all, unit, other_half, added, others)

    normed_grad = row_sum
    residual_part, feed_terms = rms_backward(residual, feed_gain, normed_grad)
    residual_grad = f32(upstream_mine) + residual_part
    feed_gain_grad = jnp.sum(feed_terms, axis=0)
    residual_mine = low(residual_grad)
    mix_sums = [after(mixes[1], residual_mine)]
    for s in range(2, dp_parts):
        mix_sums.append(low(f32(onward(mix_sums[-1])) + f32(mixes[s])))
    layer_share = low(residual + f32(onward(mix_sums[-1])) + f32(mixes[0]))

    residual_pieces = plane_gather(residual_mine, quick, expert_parts)
    residual_low = jnp.concatenate(residual_pieces, axis=0)

    if quick:
        far3 = expert_grads(3, True, None, residual_mine)
        far2 = expert_grads(2, True, None, far3, residual_pieces[1])
        near3 = expert_grads(3, False, swap(far3, "ctx"), far2)
        near1 = expert_grads(1, False, swap(far2, "ctx"), near3, mix_sums[1])
        diagonal, first = plane_hop(near3, 0), plane_hop(near1, 0)
        last = near1
    else:
        plane_grads = [
            jnp.concatenate([expert_grads(r, h, None, residual_mine) for h in (False, True)], axis=0)
            for r in range(expert_parts)
        ]
        last = plane_grads[-1]

    heads_grad_slots = low(
        lax.dot_general(residual_low, out_weight, contract_cols, preferred_element_type=jnp.float32)
    )
    heads_grad = heads_grad_slots if quick else from_slots(heads_grad_slots, order)
    out_weight_grad = lax.dot_general(
        heads_slots, residual_low, contract_rows, preferred_element_type=jnp.float32
    )
    out_weight_grad = low(out_weight_grad)
    if ctx_parts == 2:
        out_half = core_half(out_weight_grad, ctx_index)
    query_low, key_grads, value_grads, query_gain_grad = attend_back(
        own, queries, keys, keys.T, values, lse, heads, heads_grad, pre, query_gain_row, cosine, sine,
        sequel_rows, prompt_total, [last, out_weight_grad],
    )
    if quick:
        near2 = expert_grads(2, False, diagonal, query_low, mix_sums[2])
        near0 = expert_grads(0, False, first, near2, layer_share)
        key_grads = after(key_grads, diagonal)
    else:
        own_grads = lax.psum(
            low(cube_scatter(plane_grads, "expert", expert_parts, cube_bits(expert_parts))), "ctx"
        )
        width = down_weight.shape[1]
        gate_up_grad, down_grad = f32(own_grads[:, : 2 * width])[None], f32(own_grads[:, 2 * width :].T)[None]
        layer_pieces = plane_gather(layer_share, quick, expert_parts)
    coef_all = from_slots(
        after(jnp.concatenate(coefs, axis=0), query_low), owners
    )
    router_grad = jnp.dot(
        jnp.dot(f32(xt_all), coef_all, precision=HIGHEST), f32(lane_hot).T, precision=HIGHEST
    )
    kv_grads = low(jnp.concatenate([key_grads * (1.0 / LOG2E), value_grads], axis=1))
    kv_sum = ring_scatter(
        [
            jnp.concatenate([lax.dynamic_slice_in_dim(kv_grads, a, n, 0) for a, n in spans(s)], axis=0)
            for s in range(ctx_parts)
        ],
        "ctx",
        ctx_parts,
    )
    key_turned = turn(kv_sum[:, :head_dim], cosine, -sine)
    key_pre_grad, key_terms = rms_backward(key_pre, key_gain, key_turned)
    key_gain_grad = jnp.sum(key_terms, axis=0)
    low_grads = jnp.concatenate([query_low, low(key_pre_grad), low(kv_sum[:, head_dim:])], axis=1)
    hidden_grad = low(
        lax.dot_general(
            to_slots(low_grads, order), qkv_weight, contract_cols, preferred_element_type=jnp.float32
        )
    )
    hidden_grad_mine, hidden_near = plane_scatter(hidden_grad, quick, expert_parts, *([near0] if quick else []))
    if quick:
        far1 = expert_grads(1, True, swap(near2, "ctx"), hidden_near)
        layer_pieces = plane_gather(after(layer_share, hidden_grad_mine), quick, expert_parts)
        far0 = expert_grads(0, True, plane_hop(far1, 0))
        expert_outs = unpacked(core, near0, swap(far0, "ctx"), 0, [])
        gate_up_grad, down_grad = unpacked(core, far0, swap(near0, "ctx"), 1, expert_outs)
    query_grad = lax.dot_general(hidden, query_low, contract_rows, preferred_element_type=jnp.float32)
    kv_grad = lax.dot_general(hidden, low_grads[:, query_width:], contract_rows, preferred_element_type=jnp.float32)
    input_part, attention_terms = rms_backward(tokens_mine, attention_gain, hidden_grad_mine)
    attention_gain_grad = jnp.sum(attention_terms, axis=0)
    input_share = low(residual_grad + input_part)

    query_grad, kv_grad = low(query_grad), low(kv_grad)
    if ctx_parts == 2:
        halves = (out_half, core_half(query_grad, ctx_index), core_half(kv_grad, ctx_index))
        out_half, query_half, kv_half = lax.psum(halves, "dp")
        out_total, query_total = (f32(both_halves(h, ctx_index)) for h in (out_half, query_half))
    else:
        out_total, query_total = (f32(lax.psum(g, ("ctx", "dp"))) for g in (out_weight_grad, query_grad))
    if quick:
        half = model_width // 2
        kv_slots = jnp.concatenate(plane_gather(kv_half, quick, expert_parts), axis=0)
        kv_half = jnp.concatenate(
            [
                lax.dynamic_slice(kv_slots, (slot_of[j] * half, part * head_dim), (half, head_dim))
                for part in range(2)
                for j in range(KV)
            ],
            axis=1,
        )
        kv_whole = both_halves(kv_half, ctx_index)
        kv_outs = [f32(kv_whole[:, : KV * head_dim]), f32(kv_whole[:, KV * head_dim :])]
    else:
        kv_total = lax.psum(kv_grad, ("ctx", "dp"))
        kv_outs = []
        for part in range(2):
            whole = lax.dynamic_update_slice_in_dim(
                jnp.zeros((model_width, KV * head_dim), jnp.bfloat16),
                kv_total[:, part * head_dim : (part + 1) * head_dim],
                kv_first * head_dim,
                1,
            )
            kv_outs.append(f32(lax.psum(whole, "expert")))
    everywhere = ("ctx", "expert", "dp")
    smalls = [router_grad, feed_gain_grad, attention_gain_grad, query_gain_grad, key_gain_grad]
    small = jnp.concatenate([g.reshape(-1, 128) for g in smalls], axis=0)
    totals = butterfly(after(small, far0) if quick else small, everywhere)
    small_totals, at = [], 0
    for g in smalls:
        small_totals.append(totals[at : at + g.size // 128].reshape(g.shape))
        at += g.size // 128
    router_total, feed_total, attention_total, query_gain_total, key_gain_total = small_totals
    layer_out, input_out = (
        place_rows(pieces, quick, order, slot_of, prompt_rows, sequel_rows)
        for pieces in (layer_pieces, plane_gather(input_share, quick, expert_parts))
    )
    return (
        *layer_out,
        *input_out,
        attention_total,
        query_total,
        kv_outs[0],
        kv_outs[1],
        query_gain_total.reshape(head_dim),
        key_gain_total,
        out_total,
        feed_total,
        router_total,
        gate_up_grad,
        down_grad,
    )


def solution(mesh):
    placed = (
        P("dp", "ctx", None),
        P("dp", None, "ctx", None),
        P(),
        P(None, "expert"),
        P(),
        P(),
        P(),
        P(),
        P("expert", None),
        P(),
        P(),
        P(("expert", "dp"), None, None),
        P(("expert", "dp"), None, None),
        P("dp", "ctx", None),
        P("dp", None, "ctx", None),
        P("dp", "ctx", None),
        P("dp", None, "ctx", None),
    )
    return jax.shard_map(
        on_device,
        mesh=mesh,
        in_specs=placed,
        out_specs=(
            P("dp", "ctx", None),
            P("dp", None, "ctx", None),
            P("dp", "ctx", None),
            P("dp", None, "ctx", None),
            P(),
            P(None, "expert"),
            P(),
            P(),
            P(),
            P(),
            P("expert", None),
            P(),
            P(),
            P(("expert", "dp"), None, None),
            P(("expert", "dp"), None, None),
        ),
        check_vma=False,
    )
```
